32 devices in a mesh: batch: 2 (over y), tm: 8 (over z, x), mp: 2 (over core).
Axes of the slice: x: 2, y: 2, z: 4, core: 2. Of those that a mesh axis runs over, the one named last changes fastest.
Arguments:
- input_signal: bfloat16 [2, 1024, 1536], P('batch', 'tm'), may hold values from -6 to 6
- standardize_factor: float32 [1536], replicated, may hold values from 0.1 to 1.9
- triple_projection: bfloat16 [3, 1536, 768], P(None, None, 'mp'), may hold values from -0.15625 to 0.15625
- score_sharpening: float32 [8], P('mp'), may hold values from 1 to 3.5
- final_projection: bfloat16 [768, 1536], P('mp'), may hold values from -0.21875 to 0.21875
- filter_taps: float32 [31, 1536], replicated, may hold values from -1.2 to 1.2
- mixture_adjoint: bfloat16 [2, 1024, 1536], P('batch', 'tm'), may hold values from -6 to 6
Outputs:
- sublayer_result: bfloat16 [2, 1024, 1536], P('batch', 'tm')
- signal_adjoint: bfloat16 [2, 1024, 1536], P('batch', 'tm')
- filter_adjoint: float32 [31, 1536], P(None, ('batch', 'tm'))
- amplifier_adjoint: float32 [1536], P(('batch', 'tm'))
The draws below stay inside these ranges and needn't reach their ends.
All inputs are finite; a program needn't handle non-finite values.
Results may differ from the reference program's by a relative error of at most 0.015.
Values may be sent and summed in bfloat16 or wider, within the bound.
A program may use at most 128 MiB of HBM per device.

```python
import math
import jax
import jax.numpy as jnp
from jax import lax

D = 1536
FOCUS_CHANNELS = 8
HEAD_SIZE = 96
KERNEL = 31
SEQ = 1024
UTTERANCES = 2


def with_spikes(entries, stream_key, source, target, parts, factor):
    def block_of(dim):
        return (jnp.arange(entries.shape[dim]) // (entries.shape[dim] // parts)).reshape((-1,) + (1,) * (entries.ndim - 1 - dim))

    first = jax.random.permutation(stream_key, parts)[block_of(target)]
    second = (block_of(target) + parts // 2) % parts
    return jnp.where((block_of(source) == first) | (block_of(source) == second), factor * entries, entries)


def steps_of(stream_key, shape, split, smallest, top_value):
    gain = 1.0
    for axis_at, blocks in split:
        heights = jax.random.uniform(jax.random.fold_in(jax.random.fold_in(stream_key, 6), axis_at), (blocks,), jnp.float32, smallest / len(split), top_value / len(split))
        gain = gain * jnp.repeat(jnp.exp(heights), shape[axis_at] // blocks).reshape((-1,) + (1,) * (len(shape) - 1 - axis_at))
    return gain


def gaussian(key, shape, width, bound, shards=(), kind=jnp.bfloat16):
    entries = jax.random.normal(key, shape, jnp.float32) * width
    if len(shards) > 0:
        entries = steps_of(key, shape, shards, -0.22, 0.18) * entries
    return jnp.clip(entries, min=-bound, max=bound).astype(kind)


def noise_with(stream_key, shape, spread, bound, cuts, heavy, dtype=jnp.bfloat16):
    array = spread * jax.random.normal(stream_key, shape, jnp.float32)
    if cuts:
        array = array * steps_of(stream_key, shape, cuts, -0.22, 0.18)
    return jnp.clip(with_spikes(array, jax.random.fold_in(stream_key, 3), *heavy), -bound, bound).astype(dtype)


def setup_inputs(seed: int = 0) -> dict:
    splits = jax.random.split(jax.random.key(seed), 8)
    return {
        "input_signal": gaussian(splits[0], (UTTERANCES, SEQ, D), 1.0, 6.0, ((0, 2), (1, 8))),
        "standardize_factor": jnp.clip(1.0 + 0.18 * jax.random.normal(splits[1], (D,), jnp.float32), 0.1, 1.9),
        "triple_projection": gaussian(splits[2], (3, D, FOCUS_CHANNELS * HEAD_SIZE), D ** -0.5, 0.15625, ((2, 2),)),
        "score_sharpening": jnp.clip(jnp.exp(math.log(3.5) - 1.25276297 * jax.random.uniform(splits[3], (FOCUS_CHANNELS,), jnp.float32) ** steps_of(splits[3], (FOCUS_CHANNELS,), ((0, 2),), -0.2, 0.2)), 1.0, 3.5),
        "final_projection": gaussian(splits[4], (FOCUS_CHANNELS * HEAD_SIZE, D), (FOCUS_CHANNELS * HEAD_SIZE) ** -0.5, 0.21875, ((0, 2),)),
        "filter_taps": gaussian(splits[5], (KERNEL, D), 0.2, 1.2, (), jnp.float32),
        "mixture_adjoint": noise_with(splits[6], (UTTERANCES, SEQ, D), 1.0, 6.0, ((0, 2), (1, 8)), (1, 2, 8, 2.0)),
    }


def unit_rows(values_in):
    radius = jnp.sqrt(lax.optimization_barrier(jnp.mean(values_in * values_in, axis=-1, keepdims=True)) + 1e-06)
    return (values_in / radius, radius)

def rounded(values_in):
    return lax.optimization_barrier(values_in.astype(jnp.bfloat16)).astype(jnp.float32)

def solo_recording(signal_pieces, standardize_factor, triple_projection, score_sharpening, final_projection, filter_taps, adjoint_slices):
    reach = KERNEL // 2
    inputs = signal_pieces.astype(jnp.float32)
    centred = inputs - lax.optimization_barrier(jnp.mean(inputs, axis=-1, keepdims=True))
    variance = lax.optimization_barrier(jnp.mean(centred * centred, axis=-1, keepdims=True))
    inverse_std = 1.0 / jnp.sqrt(variance + 1e-05)
    incoming_entries = centred * inverse_std
    normed = (incoming_entries * standardize_factor).astype(jnp.bfloat16)
    query = jnp.dot(normed, triple_projection[0], preferred_element_type=jnp.float32).reshape(SEQ, FOCUS_CHANNELS, HEAD_SIZE)
    key_raw = jnp.dot(normed, triple_projection[1], preferred_element_type=jnp.float32).reshape(SEQ, FOCUS_CHANNELS, HEAD_SIZE)
    value_raw = jnp.dot(normed, triple_projection[2], preferred_element_type=jnp.float32).reshape(SEQ, FOCUS_CHANNELS, HEAD_SIZE)
    normalized_probes, q_radius = unit_rows(query)
    khat, k_radius = unit_rows(key_raw)
    head_sharpening = (score_sharpening / math.sqrt(HEAD_SIZE))[None, :, None]
    probe_vectors = (normalized_probes * head_sharpening).astype(jnp.bfloat16)
    keys_f = khat.astype(jnp.bfloat16).astype(jnp.float32)
    values_f = value_raw.astype(jnp.bfloat16).astype(jnp.float32)
    queries_f = probe_vectors.astype(jnp.float32)
    incoming_adjoint = adjoint_slices.astype(jnp.float32)
    grad_pad = jnp.pad(incoming_adjoint, ((reach, reach), (0, 0)))
    grad_res = incoming_adjoint
    for tap_index in range(KERNEL):
        grad_res = grad_res + filter_taps[tap_index] * grad_pad[2 * reach - tap_index:2 * reach - tap_index + SEQ]
    grad_heads = jnp.dot(grad_res.astype(jnp.bfloat16), final_projection.T, preferred_element_type=jnp.float32)
    grad_heads = grad_heads.astype(jnp.bfloat16).reshape(SEQ, FOCUS_CHANNELS, HEAD_SIZE)
    grad_heads_f = grad_heads.astype(jnp.float32)
    block_rows = math.gcd(SEQ, 512)
    block_count = SEQ // block_rows

    def query_block(pieces):
        query_part, grad_part = pieces
        score = jnp.einsum('qhe,khe->qhk', query_part, keys_f)
        weight = jnp.exp(score)
        total = lax.optimization_barrier(jnp.sum(weight, axis=-1))
        weight_low = rounded(weight)
        numer = jnp.einsum('qhk,khe->qhe', weight_low, values_f)
        product = jnp.einsum('qhe,khe->qhk', grad_part, values_f)
        weighted = weight * product
        expect = lax.optimization_barrier(jnp.sum(weighted, axis=-1))
        first = jnp.einsum('qhk,khe->qhe', rounded(weighted), keys_f)
        second = jnp.einsum('qhk,khe->qhe', weight_low, keys_f)
        attended = (numer / total[..., None]).astype(jnp.bfloat16)
        delta = expect / total
        probe_sensitivity = (first - delta[..., None] * second) / total[..., None]
        return (attended, total, delta, probe_sensitivity)
    attended, totals, deltas, probe_sensitivity = lax.map(query_block, (queries_f.reshape(block_count, block_rows, FOCUS_CHANNELS, HEAD_SIZE), grad_heads_f.reshape(block_count, block_rows, FOCUS_CHANNELS, HEAD_SIZE)))
    attended = attended.reshape(SEQ, FOCUS_CHANNELS * HEAD_SIZE)
    totals = totals.reshape(SEQ, FOCUS_CHANNELS)
    deltas = deltas.reshape(SEQ, FOCUS_CHANNELS)
    probe_sensitivity = probe_sensitivity.reshape(SEQ, FOCUS_CHANNELS, HEAD_SIZE)
    residual = (inputs + jnp.dot(attended, final_projection, preferred_element_type=jnp.float32)).astype(jnp.bfloat16)
    res_pad = jnp.pad(residual.astype(jnp.float32), ((reach, reach), (0, 0)))
    sublayer_result = residual.astype(jnp.float32)
    filter_terms = []
    for tap_index in range(KERNEL):
        receptive_span = res_pad[tap_index:tap_index + SEQ]
        sublayer_result = sublayer_result + filter_taps[tap_index] * receptive_span
        filter_terms.append(lax.optimization_barrier(jnp.sum(incoming_adjoint * receptive_span, axis=0)))
    sublayer_result = sublayer_result.astype(jnp.bfloat16)
    filter_terms = jnp.stack(filter_terms)
    totals_t = totals.T[None]
    deltas_t = deltas.T[None]

    def key_block(pieces):
        key_part, value_part = pieces
        score = jnp.einsum('khe,qhe->khq', key_part, queries_f)
        prob = jnp.exp(score) / totals_t
        grad_v = jnp.einsum('khq,qhe->khe', rounded(prob), grad_heads_f)
        product = jnp.einsum('khe,qhe->khq', value_part, grad_heads_f)
        slope = prob * (product - deltas_t)
        grad_k = jnp.einsum('khq,qhe->khe', rounded(slope), queries_f)
        return (grad_k, grad_v)
    grad_keys, grad_values = lax.map(key_block, (keys_f.reshape(block_count, block_rows, FOCUS_CHANNELS, HEAD_SIZE), values_f.reshape(block_count, block_rows, FOCUS_CHANNELS, HEAD_SIZE)))
    grad_keys = grad_keys.reshape(SEQ, FOCUS_CHANNELS, HEAD_SIZE)
    grad_values = grad_values.reshape(SEQ, FOCUS_CHANNELS, HEAD_SIZE)
    sharpened_sensitivity = probe_sensitivity * head_sharpening
    query_grad = (sharpened_sensitivity - normalized_probes * lax.optimization_barrier(jnp.mean(sharpened_sensitivity * normalized_probes, axis=-1, keepdims=True))) / q_radius
    key_grad = (grad_keys - khat * lax.optimization_barrier(jnp.mean(grad_keys * khat, axis=-1, keepdims=True))) / k_radius
    standardized_adjoint = jnp.dot(query_grad.astype(jnp.bfloat16).reshape(SEQ, FOCUS_CHANNELS * HEAD_SIZE), triple_projection[0].T, preferred_element_type=jnp.float32)
    standardized_adjoint = standardized_adjoint + jnp.dot(key_grad.astype(jnp.bfloat16).reshape(SEQ, FOCUS_CHANNELS * HEAD_SIZE), triple_projection[1].T, preferred_element_type=jnp.float32)
    standardized_adjoint = standardized_adjoint + jnp.dot(grad_values.astype(jnp.bfloat16).reshape(SEQ, FOCUS_CHANNELS * HEAD_SIZE), triple_projection[2].T, preferred_element_type=jnp.float32)
    amplifier_terms = lax.optimization_barrier(jnp.sum(standardized_adjoint * incoming_entries, axis=0))
    scaled = standardized_adjoint * standardize_factor
    frame_back = (scaled - lax.optimization_barrier(jnp.mean(scaled, axis=-1, keepdims=True)) - incoming_entries * lax.optimization_barrier(jnp.mean(scaled * incoming_entries, axis=-1, keepdims=True))) * inverse_std
    signal_adjoint = (grad_res + frame_back).astype(jnp.bfloat16)
    return (sublayer_result, signal_adjoint, filter_terms, amplifier_terms)

def reference(input_signal, standardize_factor, triple_projection, score_sharpening, final_projection, filter_taps, mixture_adjoint):
    mixed_list = []
    grad_list = []
    filter_adjoint = jnp.zeros((KERNEL, D), jnp.float32)
    amplifier_adjoint = jnp.zeros((D,), jnp.float32)
    for recording_number in range(UTTERANCES):
        sublayer_result, signal_adjoint, filter_terms, amplifier_terms = solo_recording(input_signal[recording_number], standardize_factor, triple_projection, score_sharpening, final_projection, filter_taps, mixture_adjoint[recording_number])
        mixed_list.append(sublayer_result)
        grad_list.append(signal_adjoint)
        filter_adjoint = filter_adjoint + filter_terms
        amplifier_adjoint = amplifier_adjoint + amplifier_terms
    return (jnp.stack(mixed_list), jnp.stack(grad_list), filter_adjoint, amplifier_adjoint)
```

```python
import math

import jax
import jax.numpy as jnp
from jax import lax
from jax.experimental import pallas as pl
from jax.experimental.pallas import tpu as pltpu
from jax.sharding import PartitionSpec as P

KERNEL = 31


def extended(cells, sides, width):
    for axis, dim in sides:
        count = lax.axis_size(axis)
        ends = count - 1
        head = lax.slice_in_dim(cells, 0, width, axis=dim)
        tail = lax.slice_in_dim(cells, cells.shape[dim] - width, cells.shape[dim], axis=dim)
        cells = jnp.concatenate(
            [
                lax.ppermute(tail, axis, [(i, (i + 1) % count) for i in range(ends)]),
                cells,
                lax.ppermute(head, axis, [((i + 1) % count, i) for i in range(ends)]),
            ],
            axis=dim,
        )
    return cells


def time_rims(field):
    return extended(field, (("tm", 1),), KERNEL // 2)


def heads_total(partial_sum):
    return lax.psum(partial_sum.astype(jnp.bfloat16), "mp").astype(jnp.float32)


def unit_rows(values_in):
    radius = jnp.sqrt(jnp.mean(values_in * values_in, axis=-1, keepdims=True) + 1e-06)
    return (values_in / radius, radius)


def local(
    input_signal,
    standardize_factor,
    triple_projection,
    score_sharpening,
    final_projection,
    filter_taps,
    mixture_adjoint,
):
    rows = input_signal.shape[1]
    resident_subspaces = score_sharpening.shape[0]
    head_breadth = triple_projection.shape[2] // resident_subspaces
    flat_width = resident_subspaces * head_breadth
    taps = filter_taps.shape[0]
    reach = taps // 2
    inputs = input_signal[0].astype(jnp.float32)
    centred = inputs - jnp.mean(inputs, axis=-1, keepdims=True)
    variance = jnp.mean(centred * centred, axis=-1, keepdims=True)
    inverse_std = 1.0 / jnp.sqrt(variance + 1e-05)
    incoming_entries = centred * inverse_std
    normed = (incoming_entries * standardize_factor).astype(jnp.bfloat16)
    query = jnp.dot(normed, triple_projection[0], preferred_element_type=jnp.float32).reshape(
        rows, resident_subspaces, head_breadth
    )
    key_raw = jnp.dot(normed, triple_projection[1], preferred_element_type=jnp.float32).reshape(
        rows, resident_subspaces, head_breadth
    )
    value_raw = jnp.dot(normed, triple_projection[2], preferred_element_type=jnp.float32).reshape(
        rows, resident_subspaces, head_breadth
    )
    normalized_probes, q_radius = unit_rows(query)
    khat, k_radius = unit_rows(key_raw)
    head_sharpening = (score_sharpening / math.sqrt(head_breadth))[None, :, None]
    probe_vectors = (normalized_probes * head_sharpening).astype(jnp.bfloat16)
    keys_local = khat.astype(jnp.bfloat16)
    values_local = value_raw.astype(jnp.bfloat16)
    incoming_adjoint = mixture_adjoint[0].astype(jnp.float32)
    grad_pad = time_rims(mixture_adjoint)[0].astype(jnp.float32)
    grad_res = incoming_adjoint
    for tap_index in range(taps):
        grad_res = (
            grad_res
            + filter_taps[tap_index]
            * grad_pad[2 * reach - tap_index : 2 * reach - tap_index + rows]
        )
    grad_heads = jnp.dot(
        grad_res.astype(jnp.bfloat16), final_projection.T, preferred_element_type=jnp.float32
    )
    grad_heads = grad_heads.astype(jnp.bfloat16).reshape(rows, resident_subspaces, head_breadth)
    zeros_rows = jnp.zeros((rows, resident_subspaces), jnp.float32)
    zeros_full = jnp.zeros((rows, resident_subspaces, head_breadth), jnp.float32)
    start_state = (zeros_rows, zeros_full, zeros_rows, zeros_full, zeros_full)
    key_flat = keys_local.reshape(rows, flat_width)
    value_flat = values_local.reshape(rows, flat_width)
    carry = start_state
    key_piece = lax.all_gather(key_flat, "tm", axis=0, tiled=True)
    value_piece = lax.all_gather(value_flat, "tm", axis=0, tiled=True)
    piece_rows = key_piece.shape[0]
    block_rows = math.gcd(piece_rows, 512)
    block_count = piece_rows // block_rows
    key_blocks = key_piece.reshape(block_count, block_rows, resident_subspaces, head_breadth)
    value_blocks = value_piece.reshape(block_count, block_rows, resident_subspaces, head_breadth)

    def step(state, blocks):
        totals, numer, expect, first, second = state
        key_block, value_block = blocks
        score = jnp.einsum(
            "qhe,khe->qhk", probe_vectors, key_block, preferred_element_type=jnp.float32
        )
        weight = jnp.exp(score)
        weight_low = weight.astype(jnp.bfloat16)
        numer = numer + jnp.einsum(
            "qhk,khe->qhe", weight_low, value_block, preferred_element_type=jnp.float32
        )
        product = jnp.einsum(
            "qhe,khe->qhk", grad_heads, value_block, preferred_element_type=jnp.float32
        )
        weighted = weight * product
        first = first + jnp.einsum(
            "qhk,khe->qhe",
            weighted.astype(jnp.bfloat16),
            key_block,
            preferred_element_type=jnp.float32,
        )
        second = second + jnp.einsum(
            "qhk,khe->qhe", weight_low, key_block, preferred_element_type=jnp.float32
        )
        totals = totals + jnp.sum(weight, axis=-1)
        expect = expect + jnp.sum(weighted, axis=-1)
        return ((totals, numer, expect, first, second), None)

    carry, _ = lax.scan(step, carry, (key_blocks, value_blocks))
    totals, numer, expect, first, second = carry
    attended = (numer / totals[..., None]).astype(jnp.bfloat16)
    deltas = expect / totals
    probe_sensitivity = (first - deltas[..., None] * second) / totals[..., None]
    partial_out = jnp.dot(
        attended.reshape(rows, flat_width), final_projection, preferred_element_type=jnp.float32
    )
    residual = (inputs + heads_total(partial_out)).astype(jnp.bfloat16)
    res_pad = time_rims(residual[None])[0].astype(jnp.float32)
    sublayer_result = residual.astype(jnp.float32)
    filter_pieces = []
    for tap_index in range(taps):
        receptive_span = res_pad[tap_index : tap_index + rows]
        sublayer_result = sublayer_result + filter_taps[tap_index] * receptive_span
        filter_pieces.append(jnp.sum(incoming_adjoint * receptive_span, axis=0))
    sublayer_result = sublayer_result.astype(jnp.bfloat16)
    filter_terms = jnp.stack(filter_pieces)
    carry = (zeros_full, zeros_full)
    query_piece = lax.all_gather(probe_vectors.reshape(rows, flat_width), "tm", axis=0, tiled=True)
    grad_piece = lax.all_gather(grad_heads.reshape(rows, flat_width), "tm", axis=0, tiled=True)
    total_piece = lax.all_gather(totals.astype(jnp.bfloat16), "tm", axis=0, tiled=True).astype(
        jnp.float32
    )
    delta_piece = lax.all_gather(deltas.astype(jnp.bfloat16), "tm", axis=0, tiled=True).astype(
        jnp.float32
    )
    piece_rows = query_piece.shape[0]
    block_rows = math.gcd(piece_rows, 512)
    block_count = piece_rows // block_rows
    query_blocks = query_piece.reshape(block_count, block_rows, resident_subspaces, head_breadth)
    grad_blocks = grad_piece.reshape(block_count, block_rows, resident_subspaces, head_breadth)
    total_blocks = total_piece.reshape(block_count, block_rows, resident_subspaces)
    delta_blocks = delta_piece.reshape(block_count, block_rows, resident_subspaces)

    def step(state, blocks):
        key_sum, value_sum = state
        query_block, grad_block, total_block, delta_block = blocks
        score = jnp.einsum(
            "khe,qhe->khq", keys_local, query_block, preferred_element_type=jnp.float32
        )
        prob = jnp.exp(score) / total_block.T[None]
        value_sum = value_sum + jnp.einsum(
            "khq,qhe->khe",
            prob.astype(jnp.bfloat16),
            grad_block,
            preferred_element_type=jnp.float32,
        )
        product = jnp.einsum(
            "khe,qhe->khq", values_local, grad_block, preferred_element_type=jnp.float32
        )
        slope = prob * (product - delta_block.T[None])
        key_sum = key_sum + jnp.einsum(
            "khq,qhe->khe",
            slope.astype(jnp.bfloat16),
            query_block,
            preferred_element_type=jnp.float32,
        )
        return ((key_sum, value_sum), None)

    carry, _ = lax.scan(step, carry, (query_blocks, grad_blocks, total_blocks, delta_blocks))
    grad_keys, grad_values = carry
    sharpened_sensitivity = probe_sensitivity * head_sharpening
    query_grad = (
        sharpened_sensitivity
        - normalized_probes
        * jnp.mean(sharpened_sensitivity * normalized_probes, axis=-1, keepdims=True)
    ) / q_radius
    key_grad = (grad_keys - khat * jnp.mean(grad_keys * khat, axis=-1, keepdims=True)) / k_radius
    normed_part = jnp.dot(
        query_grad.astype(jnp.bfloat16).reshape(rows, flat_width),
        triple_projection[0].T,
        preferred_element_type=jnp.float32,
    )
    normed_part = normed_part + jnp.dot(
        key_grad.astype(jnp.bfloat16).reshape(rows, flat_width),
        triple_projection[1].T,
        preferred_element_type=jnp.float32,
    )
    normed_part = normed_part + jnp.dot(
        grad_values.astype(jnp.bfloat16).reshape(rows, flat_width),
        triple_projection[2].T,
        preferred_element_type=jnp.float32,
    )
    standardized_adjoint = heads_total(normed_part)
    amplifier_terms = jnp.sum(standardized_adjoint * incoming_entries, axis=0)
    scaled = standardized_adjoint * standardize_factor
    frame_back = (
        scaled
        - jnp.mean(scaled, axis=-1, keepdims=True)
        - incoming_entries * jnp.mean(scaled * incoming_entries, axis=-1, keepdims=True)
    ) * inverse_std
    signal_adjoint = (grad_res + frame_back).astype(jnp.bfloat16)
    kernel_part, gain_part = (
        lax.psum_scatter(filter_terms, ("batch", "tm"), scatter_dimension=1, tiled=True),
        lax.psum_scatter(amplifier_terms, ("batch", "tm"), scatter_dimension=0, tiled=True),
    )
    return (sublayer_result[None], signal_adjoint[None], kernel_part, gain_part)


F32 = jnp.float32
BF16 = jnp.bfloat16
MESH = pl.DeviceIdType.MESH
PAD = 16
LANES = 128


def fits(mesh):
    return mesh.shape["tm"] == 8 and mesh.shape["batch"] == 2 and mesh.shape["mp"] == 2


def dot(a, b, ca, cb):
    return lax.dot_general(a, b, (((ca,), (cb,)), ((), ())), preferred_element_type=F32)


def fused_kernel(
    x_ref, gain_ref, w_ref, sharp_ref, fp_ref, taps_ref, m_ref,
    sub_ref, sig_ref, filt_ref, amp_ref,
    unit, invstd, qhat, khat, qrad, krad,
    kvs, qs, gs, kvr, qr, gr,
    probs, prods, atts, attr, dqs, dqr, dkvs, dkvr,
    mpad, rpad, hm, hr, resid, gres, pos, por, nps, npr,
    fl, fs, fr, ams, amr,
    kv_ss, kv_rs, q_ss, q_rs, g_ss, g_rs, at_ss, at_rs, dq_ss, dq_rs, dk_ss, dk_rs,
    hm_ss, hm_rs, hr_ss, hr_rs, ex_ss, ex_rs, f_ss, f_rs, a_ss, a_rs,
):
    batch = lax.axis_index("batch")
    t = lax.axis_index("tm")
    c = lax.axis_index("mp")
    T = lax.axis_size("tm")
    B = lax.axis_size("batch")
    H, E, R = qhat.shape
    D = x_ref.shape[2]
    half = D // 2
    chunks = half // LANES
    taps = taps_ref.shape[0]
    reach = taps // 2
    p = lax.rem(t, H)
    base = t - p
    sib = 1 - c
    nxt = lax.rem(t + 1, T)
    prv = lax.rem(t + T - 1, T)
    flat = batch * T + t
    N = B * T

    def rcopy(src, dst, ss, rs, **dev):
        return pltpu.make_async_remote_copy(
            src_ref=src, dst_ref=dst, send_sem=ss, recv_sem=rs,
            device_id=dev, device_id_type=MESH,
        )

    def lanes(core, i=0, width=None):
        return pl.ds(pl.multiple_of(core * half + i * LANES, LANES), width or half)

    barrier = pltpu.get_barrier_semaphore()

    def greet(o, carry):
        d = lax.rem(flat * 2 + c + o, N * 2)
        pl.semaphore_signal(
            barrier, inc=1,
            device_id={"batch": d // (2 * T), "tm": lax.rem(d // 2, T), "mp": lax.rem(d, 2)},
            device_id_type=MESH,
        )
        return carry

    lax.fori_loop(1, N * 2, greet, 0)

    x = x_ref[0].astype(F32)
    cen = x - jnp.mean(x, axis=-1, keepdims=True)
    inv = 1.0 / jnp.sqrt(jnp.mean(cen * cen, axis=-1, keepdims=True) + 1e-05)
    u = cen * inv
    unit[...] = u
    invstd[...] = inv
    normed = (u * gain_ref[...]).astype(BF16)

    kt = jnp.transpose(dot(normed, w_ref[1], 1, 0))
    vt = jnp.transpose(dot(normed, w_ref[2], 1, 0))
    for h in range(H):
        kh = kt[E * h : E * h + E]
        rad = jnp.sqrt(jnp.mean(kh * kh, axis=0, keepdims=True) + 1e-06)
        kh = kh / rad
        khat[h] = kh
        krad[h] = rad
        kvs[h, 0:E] = kh.astype(BF16)
        kvs[h, E : 2 * E] = vt[E * h : E * h + E].astype(BF16)

    pl.semaphore_wait(barrier, N * 2 - 1)

    to_next = rcopy(m_ref.at[0, pl.ds(R - PAD, PAD), lanes(c)], hm.at[0], hm_ss.at[0], hm_rs.at[0], tm=nxt)
    to_prev = rcopy(m_ref.at[0, pl.ds(0, PAD), lanes(c)], hm.at[1], hm_ss.at[1], hm_rs.at[1], tm=prv)
    to_next.start()
    to_prev.start()
    kv_copies = []
    for o in (4, 3, 5, 2, 6, 1, 7):
        d = lax.rem(t + o, T)
        kv_copies.append(rcopy(kvs.at[lax.rem(d, H)], kvr.at[t], kv_ss.at[o], kv_rs.at[o], tm=d))
        kv_copies[-1].start()
    kvr[t] = kvs[p]

    qt = jnp.transpose(dot(normed, w_ref[0], 1, 0))
    for h in range(H):
        qh = qt[E * h : E * h + E]
        rad = jnp.sqrt(jnp.mean(qh * qh, axis=0, keepdims=True) + 1e-06)
        qh = qh / rad
        qhat[h] = qh
        qrad[h] = rad
        qs[h] = (qh * (sharp_ref[h] / math.sqrt(E))).astype(BF16)
    q_copies = []
    for o in range(1, H):
        d = lax.rem(p + o, H)
        q_copies.append(rcopy(qs.at[d], qr.at[p], q_ss.at[o], q_rs.at[o], tm=base + d))
        q_copies[-1].start()
    qr[p] = qs[p]

    to_next.wait_recv()
    to_prev.wait_recv()

    def fill(pad, halo, body):
        def one(i, carry):
            ln = pl.ds(pl.multiple_of(i * LANES, LANES), LANES)
            pad[i, 0:PAD, :] = jnp.where(t > 0, halo[0, :, ln].astype(F32), 0.0)
            pad[i, PAD + R : 2 * PAD + R, :] = jnp.where(t < T - 1, halo[1, :, ln].astype(F32), 0.0)
            body(i, ln)
            return carry

        lax.fori_loop(0, chunks, one, 0)

    def back(i, ln):
        mpad[i, PAD : PAD + R, :] = m_ref[0, :, lanes(c, i, LANES)].astype(F32)
        acc = mpad[i, PAD : PAD + R, :]
        for j in range(taps):
            s = PAD + reach - j
            acc = acc + taps_ref[j : j + 1, lanes(c, i, LANES)] * mpad[i, s : s + R, :]
        gres[c, :, ln] = acc.astype(BF16)

    fill(mpad, hm, back)
    gex = rcopy(gres.at[c], gres.at[c], ex_ss.at[0], ex_rs.at[0], mp=sib)
    gex.start()
    for o in range(H - 1):
        q_copies[o].wait_recv()
    for cp in kv_copies:
        cp.wait_recv()

    QT = jnp.concatenate([qr[i] for i in range(H)], axis=1)
    total = jnp.zeros((1, H * R), F32)
    att = jnp.zeros((E, H * R), F32)
    pairs = T // 2

    def pair(i, lo):
        return jnp.concatenate([kvr[2 * i, lo : lo + E], kvr[2 * i + 1, lo : lo + E]], axis=1)

    def forward(i, state):
        total, att = state
        w = jnp.exp(dot(pair(i, 0), QT, 0, 0))
        probs[i] = w
        return (
            total + jnp.sum(w, axis=0, keepdims=True),
            att + dot(pair(i, E), w.astype(BF16), 1, 0),
        )

    total, att = lax.fori_loop(0, pairs, forward, (total, att))
    inv_total = 1.0 / total
    att = (att * inv_total).astype(BF16)
    for i in range(H):
        atts[i] = att[:, R * i : R * i + R]
    at_copies = []
    for o in range(1, H):
        d = lax.rem(p + o, H)
        at_copies.append(rcopy(atts.at[d], attr.at[p], at_ss.at[o], at_rs.at[o], tm=base + d))
        at_copies[-1].start()
    attr[p] = atts[p]

    gex.wait_recv()
    gt = dot(fp_ref[:, 0:half], gres[0], 1, 1) + dot(fp_ref[:, half:D], gres[1], 1, 1)
    for h in range(H):
        gs[h] = gt[E * h : E * h + E].astype(BF16)
    g_copies = []
    for o in range(1, H):
        d = lax.rem(p + o, H)
        g_copies.append(rcopy(gs.at[d], gr.at[p], g_ss.at[o], g_rs.at[o], tm=base + d))
        g_copies[-1].start()
    gr[p] = gs[p]

    for cp in at_copies:
        cp.wait_recv()
    attended = attr[...].reshape(H * E, R)
    pos[...] = dot(attended, fp_ref[:, lanes(sib)], 0, 0).astype(BF16)
    pex = rcopy(pos, por, ex_ss.at[1], ex_rs.at[1], mp=sib)
    pex.start()
    own = x_ref[0, :, lanes(c)].astype(F32) + dot(attended, fp_ref[:, lanes(c)], 0, 0)
    pex.wait_recv()
    own = (own + por[...].astype(F32)).astype(BF16)
    resid[...] = own
    r_next = rcopy(resid.at[pl.ds(R - PAD, PAD)], hr.at[0], hr_ss.at[0], hr_rs.at[0], tm=nxt)
    r_prev = rcopy(resid.at[pl.ds(0, PAD)], hr.at[1], hr_ss.at[1], hr_rs.at[1], tm=prv)
    r_next.start()
    r_prev.start()

    for cp in g_copies:
        cp.wait_recv()
    GT = jnp.concatenate([gr[i] for i in range(H)], axis=1)

    def products(i, expect):
        prod = dot(pair(i, E), GT, 0, 0)
        prods[i] = prod
        return expect + jnp.sum(probs[i] * prod, axis=0, keepdims=True)

    expect = lax.fori_loop(0, pairs, products, jnp.zeros((1, H * R), F32))
    delta = expect * inv_total

    def backward(i, dq):
        prob = probs[i] * inv_total
        slope = (prob * (prods[i] - delta)).astype(BF16)
        dk = dot(QT, slope, 1, 1).astype(BF16)
        dv = dot(GT, prob.astype(BF16), 1, 1).astype(BF16)
        for s in range(2):
            dkvs[2 * i + s, 0:E] = dk[:, R * s : R * s + R]
            dkvs[2 * i + s, E : 2 * E] = dv[:, R * s : R * s + R]
        return dq + dot(pair(i, 0), slope, 1, 0)

    dq = lax.fori_loop(0, pairs, backward, jnp.zeros((E, H * R), F32)).astype(BF16)
    for i in range(H):
        dqs[i] = dq[:, R * i : R * i + R]
    dk_copies = []
    for o in (4, 3, 5, 2, 6, 1, 7):
        d = lax.rem(t + o, T)
        dk_copies.append(rcopy(dkvs.at[d], dkvr.at[t], dk_ss.at[o], dk_rs.at[o], tm=d))
        dk_copies[-1].start()
    dkvr[t] = dkvs[t]
    dq_copies = []
    for o in range(1, H):
        d = lax.rem(p + o, H)
        dq_copies.append(rcopy(dqs.at[d], dqr.at[p], dq_ss.at[o], dq_rs.at[o], tm=base + d))
        dq_copies[-1].start()
    dqr[p] = dqs[p]

    r_next.wait_recv()
    r_prev.wait_recv()
    fl[taps:, :] = jnp.zeros((fl.shape[0] - taps, half), F32)

    def mix(i, ln):
        rpad[i, PAD : PAD + R, :] = resid[:, ln].astype(F32)
        grad = mpad[i, PAD : PAD + R, :]
        acc = rpad[i, PAD : PAD + R, :]
        for j in range(taps):
            s = PAD - reach + j
            win = rpad[i, s : s + R, :]
            acc = acc + taps_ref[j : j + 1, lanes(c, i, LANES)] * win
            fl[j : j + 1, ln] = jnp.sum(grad * win, axis=0, keepdims=True)
        sub_ref[0, :, lanes(c, i, LANES)] = acc.astype(BF16)

    fill(rpad, hr, mix)
    sex = rcopy(sub_ref.at[0, :, lanes(c)], sub_ref.at[0, :, lanes(c)], ex_ss.at[2], ex_rs.at[2], mp=sib)
    sex.start()

    width = filt_ref.shape[1]
    fs[...] = jnp.zeros(fs.shape, F32)
    for k in range(T):
        fs[k, :, 0:width] = fl[:, width * k : width * k + width]

    def filter_copy(i):
        k, m = i // 2, lax.rem(i, 2)
        return (
            (batch == c) & (t == k) & (m == c),
            rcopy(fs.at[k], fr.at[flat], f_ss.at[i], f_rs.at[flat], batch=c, tm=k, mp=m),
        )

    def filter_send(i, carry):
        mine, cp = filter_copy(i)

        @pl.when(jnp.logical_not(mine))
        def _():
            cp.start()

        return carry

    lax.fori_loop(0, 2 * T, filter_send, 0)

    @pl.when(batch == c)
    def _():
        fr[flat] = fs[t]

    for cp in dq_copies:
        cp.wait_recv()
    for cp in dk_copies:
        cp.wait_recv()
    parts = ([], [], [])
    for h in range(H):
        g = dqr[h].astype(F32) * (sharp_ref[h] / math.sqrt(E))
        hat = qhat[h]
        parts[0].append((g - hat * jnp.mean(g * hat, axis=0, keepdims=True)) / qrad[h])
        g = dkvr[h, 0:E].astype(F32)
        v = dkvr[h, E : 2 * E].astype(F32)
        for s in range(H, T, H):
            g = g + dkvr[s + h, 0:E].astype(F32)
            v = v + dkvr[s + h, E : 2 * E].astype(F32)
        hat = khat[h]
        parts[1].append((g - hat * jnp.mean(g * hat, axis=0, keepdims=True)) / krad[h])
        parts[2].append(v)
    rows = [jnp.transpose(jnp.concatenate(part, axis=0)).astype(BF16) for part in parts]
    part = dot(rows[0], w_ref[0], 1, 1) + dot(rows[1], w_ref[1], 1, 1) + dot(rows[2], w_ref[2], 1, 1)
    nps[...] = part.astype(BF16)
    nex = rcopy(nps, npr, ex_ss.at[3], ex_rs.at[3], mp=sib)
    nex.start()
    nex.wait_recv()
    z = nps[...].astype(F32) + npr[...].astype(F32)
    u = unit[...]
    amp = jnp.sum(z * u, axis=0, keepdims=True)
    ams[...] = jnp.zeros(ams.shape, F32)
    for k in range(N):
        ams[k, 0:1, 0:width] = amp[:, width * k : width * k + width]

    def amp_copy(o):
        d = lax.rem(flat + o, N)
        return rcopy(ams.at[d], amr.at[flat], a_ss.at[o], a_rs.at[o], batch=d // T, tm=lax.rem(d, T))

    def amp_send(o, carry):
        amp_copy(o).start()
        return carry

    lax.fori_loop(1, N, amp_send, 0)
    amr[flat] = ams[flat]

    s = z * gain_ref[...]
    fb = (
        s - jnp.mean(s, axis=-1, keepdims=True) - u * jnp.mean(s * u, axis=-1, keepdims=True)
    ) * invstd[...]
    for k in range(2):
        cols = slice(k * half, k * half + half)
        sig_ref[0, :, cols] = (gres[k].astype(F32) + fb[:, cols]).astype(BF16)

    def filter_wait(i, carry):
        mine = (batch == c) & (i == flat)

        @pl.when(jnp.logical_not(mine))
        def _():
            rcopy(fs.at[0], fr.at[i], f_ss.at[0], f_rs.at[i], mp=sib).wait_recv()

        return carry

    lax.fori_loop(0, N, filter_wait, 0)
    acc = fr[0]
    for k in range(1, N):
        acc = acc + fr[k]
    filt_ref[...] = acc[0:taps, 0:width]

    def amp_wait(o, carry):
        amp_copy(o).wait()
        return carry

    lax.fori_loop(1, N, amp_wait, 0)
    acc = amr[0]
    for k in range(1, N):
        acc = acc + amr[k]
    amp_ref[...] = acc[0:1, 0:width]

    def filter_sent(i, carry):
        mine, cp = filter_copy(i)

        @pl.when(jnp.logical_not(mine))
        def _():
            cp.wait_send()

        return carry

    lax.fori_loop(0, 2 * T, filter_sent, 0)
    sex.wait_recv()
    for cp in (to_next, to_prev, r_next, r_prev, gex, pex, sex, nex):
        cp.wait_send()
    for cp in kv_copies + q_copies + g_copies + at_copies + dq_copies + dk_copies:
        cp.wait_send()


def fused(x, gain, w, sharp, fp, taps, m):
    R, D = x.shape[1:]
    H = sharp.shape[0]
    E = w.shape[2] // H
    T = lax.axis_size("tm")
    N = T * lax.axis_size("batch")
    half = D // 2
    n_taps = taps.shape[0]
    width = D // N
    assert H * 2 == T and R == LANES
    v = pltpu.VMEM
    dma = pltpu.SemaphoreType.DMA
    vm = pl.BlockSpec(memory_space=pltpu.VMEM)
    sm = pl.BlockSpec(memory_space=pltpu.SMEM)
    sub, sig, filt, amp = pl.pallas_call(
        fused_kernel,
        out_shape=(
            jax.ShapeDtypeStruct((1, R, D), BF16),
            jax.ShapeDtypeStruct((1, R, D), BF16),
            jax.ShapeDtypeStruct((n_taps, width), F32),
            jax.ShapeDtypeStruct((1, width), F32),
        ),
        in_specs=[vm, vm, vm, sm, vm, vm, vm],
        out_specs=(vm, vm, vm, vm),
        scratch_shapes=[
            v((R, D), F32), v((R, 1), F32), v((H, E, R), F32), v((H, E, R), F32),
            v((H, 1, R), F32), v((H, 1, R), F32),
            v((H, 2 * E, R), BF16), v((H, E, R), BF16), v((H, E, R), BF16),
            v((T, 2 * E, R), BF16), v((H, E, R), BF16), v((H, E, R), BF16),
            v((T // 2, 2 * R, H * R), F32), v((T // 2, 2 * R, H * R), F32),
            v((H, E, R), BF16), v((H, E, R), BF16), v((H, E, R), BF16), v((H, E, R), BF16),
            v((T, 2 * E, R), BF16), v((T, 2 * E, R), BF16),
            v((half // LANES, R + 2 * PAD, LANES), F32), v((half // LANES, R + 2 * PAD, LANES), F32),
            v((2, PAD, half), BF16), v((2, PAD, half), BF16),
            v((R, half), BF16), v((2, R, half), BF16),
            v((R, half), BF16), v((R, half), BF16), v((R, D), BF16), v((R, D), BF16),
            v((n_taps + 1, half), F32), v((T, n_taps + 1, LANES), F32), v((N, n_taps + 1, LANES), F32),
            v((N, 8, LANES), F32), v((N, 8, LANES), F32),
            dma((T,)), dma((T,)), dma((H,)), dma((H,)), dma((H,)), dma((H,)),
            dma((H,)), dma((H,)), dma((H,)), dma((H,)), dma((T,)), dma((T,)),
            dma((2,)), dma((2,)), dma((2,)), dma((2,)), dma((4,)), dma((4,)),
            dma((2 * T,)), dma((N,)), dma((N,)), dma((N,)),
        ],
        compiler_params=pltpu.CompilerParams(
            collective_id=0, has_side_effects=True, vmem_limit_bytes=48 * 2**20
        ),
    )(x, gain.reshape(1, D), w, sharp, fp, taps, m)
    return sub, sig, filt, amp.reshape(width)


def solution(mesh):
    return jax.shard_map(
        fused if fits(mesh) else local,
        mesh=mesh,
        in_specs=(
            P("batch", "tm", None),
            P(),
            P(None, None, "mp"),
            P("mp"),
            P("mp", None),
            P(),
            P("batch", "tm", None),
        ),
        out_specs=(
            P("batch", "tm", None),
            P("batch", "tm", None),
            P(None, ("batch", "tm")),
            P(("batch", "tm")),
        ),
        check_vma=False,
    )
```

```python
import math

import jax
import jax.numpy as jnp
from jax import lax
from jax.experimental import pallas as pl
from jax.experimental.pallas import tpu as pltpu
from jax.sharding import PartitionSpec as P

KERNEL = 31


def extended(cells, sides, width):
    for axis, dim in sides:
        count = lax.axis_size(axis)
        ends = count - 1
        head = lax.slice_in_dim(cells, 0, width, axis=dim)
        tail = lax.slice_in_dim(cells, cells.shape[dim] - width, cells.shape[dim], axis=dim)
        cells = jnp.concatenate(
            [
                lax.ppermute(tail, axis, [(i, (i + 1) % count) for i in range(ends)]),
                cells,
                lax.ppermute(head, axis, [((i + 1) % count, i) for i in range(ends)]),
            ],
            axis=dim,
        )
    return cells


def time_rims(field):
    return extended(field, (("tm", 1),), KERNEL // 2)


def heads_total(partial_sum):
    return lax.psum(partial_sum.astype(jnp.bfloat16), "mp").astype(jnp.float32)


def unit_rows(values_in):
    radius = jnp.sqrt(jnp.mean(values_in * values_in, axis=-1, keepdims=True) + 1e-06)
    return (values_in / radius, radius)


def local(
    input_signal,
    standardize_factor,
    triple_projection,
    score_sharpening,
    final_projection,
    filter_taps,
    mixture_adjoint,
):
    rows = input_signal.shape[1]
    resident_subspaces = score_sharpening.shape[0]
    head_breadth = triple_projection.shape[2] // resident_subspaces
    flat_width = resident_subspaces * head_breadth
    taps = filter_taps.shape[0]
    reach = taps // 2
    inputs = input_signal[0].astype(jnp.float32)
    centred = inputs - jnp.mean(inputs, axis=-1, keepdims=True)
    variance = jnp.mean(centred * centred, axis=-1, keepdims=True)
    inverse_std = 1.0 / jnp.sqrt(variance + 1e-05)
    incoming_entries = centred * inverse_std
    normed = (incoming_entries * standardize_factor).astype(jnp.bfloat16)
    query = jnp.dot(normed, triple_projection[0], preferred_element_type=jnp.float32).reshape(
        rows, resident_subspaces, head_breadth
    )
    key_raw = jnp.dot(normed, triple_projection[1], preferred_element_type=jnp.float32).reshape(
        rows, resident_subspaces, head_breadth
    )
    value_raw = jnp.dot(normed, triple_projection[2], preferred_element_type=jnp.float32).reshape(
        rows, resident_subspaces, head_breadth
    )
    normalized_probes, q_radius = unit_rows(query)
    khat, k_radius = unit_rows(key_raw)
    head_sharpening = (score_sharpening / math.sqrt(head_breadth))[None, :, None]
    probe_vectors = (normalized_probes * head_sharpening).astype(jnp.bfloat16)
    keys_local = khat.astype(jnp.bfloat16)
    values_local = value_raw.astype(jnp.bfloat16)
    incoming_adjoint = mixture_adjoint[0].astype(jnp.float32)
    grad_pad = time_rims(mixture_adjoint)[0].astype(jnp.float32)
    grad_res = incoming_adjoint
    for tap_index in range(taps):
        grad_res = (
            grad_res
            + filter_taps[tap_index]
            * grad_pad[2 * reach - tap_index : 2 * reach - tap_index + rows]
        )
    grad_heads = jnp.dot(
        grad_res.astype(jnp.bfloat16), final_projection.T, preferred_element_type=jnp.float32
    )
    grad_heads = grad_heads.astype(jnp.bfloat16).reshape(rows, resident_subspaces, head_breadth)
    zeros_rows = jnp.zeros((rows, resident_subspaces), jnp.float32)
    zeros_full = jnp.zeros((rows, resident_subspaces, head_breadth), jnp.float32)
    start_state = (zeros_rows, zeros_full, zeros_rows, zeros_full, zeros_full)
    key_flat = keys_local.reshape(rows, flat_width)
    value_flat = values_local.reshape(rows, flat_width)
    carry = start_state
    key_piece = lax.all_gather(key_flat, "tm", axis=0, tiled=True)
    value_piece = lax.all_gather(value_flat, "tm", axis=0, tiled=True)
    piece_rows = key_piece.shape[0]
    block_rows = math.gcd(piece_rows, 512)
    block_count = piece_rows // block_rows
    key_blocks = key_piece.reshape(block_count, block_rows, resident_subspaces, head_breadth)
    value_blocks = value_piece.reshape(block_count, block_rows, resident_subspaces, head_breadth)

    def step(state, blocks):
        totals, numer, expect, first, second = state
        key_block, value_block = blocks
        score = jnp.einsum(
            "qhe,khe->qhk", probe_vectors, key_block, preferred_element_type=jnp.float32
        )
        weight = jnp.exp(score)
        weight_low = weight.astype(jnp.bfloat16)
        numer = numer + jnp.einsum(
            "qhk,khe->qhe", weight_low, value_block, preferred_element_type=jnp.float32
        )
        product = jnp.einsum(
            "qhe,khe->qhk", grad_heads, value_block, preferred_element_type=jnp.float32
        )
        weighted = weight * product
        first = first + jnp.einsum(
            "qhk,khe->qhe",
            weighted.astype(jnp.bfloat16),
            key_block,
            preferred_element_type=jnp.float32,
        )
        second = second + jnp.einsum(
            "qhk,khe->qhe", weight_low, key_block, preferred_element_type=jnp.float32
        )
        totals = totals + jnp.sum(weight, axis=-1)
        expect = expect + jnp.sum(weighted, axis=-1)
        return ((totals, numer, expect, first, second), None)

    carry, _ = lax.scan(step, carry, (key_blocks, value_blocks))
    totals, numer, expect, first, second = carry
    attended = (numer / totals[..., None]).astype(jnp.bfloat16)
    deltas = expect / totals
    probe_sensitivity = (first - deltas[..., None] * second) / totals[..., None]
    partial_out = jnp.dot(
        attended.reshape(rows, flat_width), final_projection, preferred_element_type=jnp.float32
    )
    residual = (inputs + heads_total(partial_out)).astype(jnp.bfloat16)
    res_pad = time_rims(residual[None])[0].astype(jnp.float32)
    sublayer_result = residual.astype(jnp.float32)
    filter_pieces = []
    for tap_index in range(taps):
        receptive_span = res_pad[tap_index : tap_index + rows]
        sublayer_result = sublayer_result + filter_taps[tap_index] * receptive_span
        filter_pieces.append(jnp.sum(incoming_adjoint * receptive_span, axis=0))
    sublayer_result = sublayer_result.astype(jnp.bfloat16)
    filter_terms = jnp.stack(filter_pieces)
    carry = (zeros_full, zeros_full)
    query_piece = lax.all_gather(probe_vectors.reshape(rows, flat_width), "tm", axis=0, tiled=True)
    grad_piece = lax.all_gather(grad_heads.reshape(rows, flat_width), "tm", axis=0, tiled=True)
    total_piece = lax.all_gather(totals.astype(jnp.bfloat16), "tm", axis=0, tiled=True).astype(
        jnp.float32
    )
    delta_piece = lax.all_gather(deltas.astype(jnp.bfloat16), "tm", axis=0, tiled=True).astype(
        jnp.float32
    )
    piece_rows = query_piece.shape[0]
    block_rows = math.gcd(piece_rows, 512)
    block_count = piece_rows // block_rows
    query_blocks = query_piece.reshape(block_count, block_rows, resident_subspaces, head_breadth)
    grad_blocks = grad_piece.reshape(block_count, block_rows, resident_subspaces, head_breadth)
    total_blocks = total_piece.reshape(block_count, block_rows, resident_subspaces)
    delta_blocks = delta_piece.reshape(block_count, block_rows, resident_subspaces)

    def step(state, blocks):
        key_sum, value_sum = state
        query_block, grad_block, total_block, delta_block = blocks
        score = jnp.einsum(
            "khe,qhe->khq", keys_local, query_block, preferred_element_type=jnp.float32
        )
        prob = jnp.exp(score) / total_block.T[None]
        value_sum = value_sum + jnp.einsum(
            "khq,qhe->khe",
            prob.astype(jnp.bfloat16),
            grad_block,
            preferred_element_type=jnp.float32,
        )
        product = jnp.einsum(
            "khe,qhe->khq", values_local, grad_block, preferred_element_type=jnp.float32
        )
        slope = prob * (product - delta_block.T[None])
        key_sum = key_sum + jnp.einsum(
            "khq,qhe->khe",
            slope.astype(jnp.bfloat16),
            query_block,
            preferred_element_type=jnp.float32,
        )
        return ((key_sum, value_sum), None)

    carry, _ = lax.scan(step, carry, (query_blocks, grad_blocks, total_blocks, delta_blocks))
    grad_keys, grad_values = carry
    sharpened_sensitivity = probe_sensitivity * head_sharpening
    query_grad = (
        sharpened_sensitivity
        - normalized_probes
        * jnp.mean(sharpened_sensitivity * normalized_probes, axis=-1, keepdims=True)
    ) / q_radius
    key_grad = (grad_keys - khat * jnp.mean(grad_keys * khat, axis=-1, keepdims=True)) / k_radius
    normed_part = jnp.dot(
        query_grad.astype(jnp.bfloat16).reshape(rows, flat_width),
        triple_projection[0].T,
        preferred_element_type=jnp.float32,
    )
    normed_part = normed_part + jnp.dot(
        key_grad.astype(jnp.bfloat16).reshape(rows, flat_width),
        triple_projection[1].T,
        preferred_element_type=jnp.float32,
    )
    normed_part = normed_part + jnp.dot(
        grad_values.astype(jnp.bfloat16).reshape(rows, flat_width),
        triple_projection[2].T,
        preferred_element_type=jnp.float32,
    )
    standardized_adjoint = heads_total(normed_part)
    amplifier_terms = jnp.sum(standardized_adjoint * incoming_entries, axis=0)
    scaled = standardized_adjoint * standardize_factor
    frame_back = (
        scaled
        - jnp.mean(scaled, axis=-1, keepdims=True)
        - incoming_entries * jnp.mean(scaled * incoming_entries, axis=-1, keepdims=True)
    ) * inverse_std
    signal_adjoint = (grad_res + frame_back).astype(jnp.bfloat16)
    kernel_part, gain_part = (
        lax.psum_scatter(filter_terms, ("batch", "tm"), scatter_dimension=1, tiled=True),
        lax.psum_scatter(amplifier_terms, ("batch", "tm"), scatter_dimension=0, tiled=True),
    )
    return (sublayer_result[None], signal_adjoint[None], kernel_part, gain_part)


F32 = jnp.float32
BF16 = jnp.bfloat16
MESH = pl.DeviceIdType.MESH
PAD = 16
LANES = 128


def fits(mesh):
    return mesh.shape["tm"] == 8 and mesh.shape["batch"] == 2 and mesh.shape["mp"] == 2


def dot(a, b, ca, cb):
    return lax.dot_general(a, b, (((ca,), (cb,)), ((), ())), preferred_element_type=F32)


def fused_kernel(
    x_in, gain_in, w_in, sharp_in, fp_in, taps_in, m_in,
    sub_ref, sig_ref, filt_ref, amp_ref,
    unit, invstd, qhat, khat, qrad, krad,
    kvs, qs, gs, kvr, qr, gr,
    probs, prods, atts, attr, dqs, dqr, dkvs, dkvr,
    mpad, rpad, hm, hr, resid, gres, pos, por, nps, npr,
    fl, fs, fr, ft, ams, amr,
    x_ref, gain_ref, w_ref, sharp_ref, fp_ref, taps_ref, m_ref, in_s,
    k_ss, k_rs, v_ss, v_rs, q_ss, q_rs, g_ss, g_rs, at_ss, at_rs, dq_ss, dq_rs, dk_ss, dk_rs,
    hm_ss, hm_rs, hr_ss, hr_rs, ex_ss, ex_rs, f_ss, f_rs, a_ss, a_rs,
):
    batch = lax.axis_index("batch")
    t = lax.axis_index("tm")
    c = lax.axis_index("mp")
    T = lax.axis_size("tm")
    B = lax.axis_size("batch")
    H, E, R = qhat.shape
    D = x_ref.shape[2]
    half = D // 2
    chunks = half // LANES
    taps = taps_ref.shape[0]
    reach = taps // 2
    p = lax.rem(t, H)
    base = t - p
    sib = 1 - c
    nxt = lax.rem(t + 1, T)
    prv = lax.rem(t + T - 1, T)
    flat = batch * T + t
    N = B * T

    def rcopy(src, dst, ss, rs, **dev):
        return pltpu.make_async_remote_copy(
            src_ref=src, dst_ref=dst, send_sem=ss, recv_sem=rs,
            device_id=dev, device_id_type=MESH,
        )

    def lanes(core, i=0, width=None):
        return pl.ds(pl.multiple_of(core * half + i * LANES, LANES), width or half)

    barrier = pltpu.get_barrier_semaphore()

    def greet(o, carry):
        d = lax.rem(flat * 2 + c + o, N * 2)
        pl.semaphore_signal(
            barrier, inc=1,
            device_id={"batch": d // (2 * T), "tm": lax.rem(d // 2, T), "mp": lax.rem(d, 2)},
            device_id_type=MESH,
        )
        return carry

    lax.fori_loop(1, N * 2, greet, 0)

    loads = {
        name: pltpu.make_async_copy(src, dst, in_s.at[i])
        for i, (name, src, dst) in enumerate((
            ("x", x_in, x_ref),
            ("gain", gain_in, gain_ref),
            ("k", w_in.at[1], w_ref.at[1]),
            ("v", w_in.at[2], w_ref.at[2]),
            ("m", m_in, m_ref),
            ("q", w_in.at[0], w_ref.at[0]),
            ("sharp", sharp_in, sharp_ref),
            ("taps", taps_in, taps_ref),
            ("fp", fp_in, fp_ref),
        ))
    }
    for load in loads.values():
        load.start()

    loads["x"].wait()
    x = x_ref[0].astype(F32)
    cen = x - jnp.mean(x, axis=-1, keepdims=True)
    inv = 1.0 / jnp.sqrt(jnp.mean(cen * cen, axis=-1, keepdims=True) + 1e-05)
    u = cen * inv
    unit[...] = u
    invstd[...] = inv
    loads["gain"].wait()
    gain = gain_ref[...].reshape(1, D)
    normed = (u * gain).astype(BF16)

    pl.semaphore_wait(barrier, N * 2 - 1)

    loads["m"].wait()
    to_next = rcopy(m_ref.at[0, pl.ds(R - PAD, PAD), lanes(c)], hm.at[0], hm_ss.at[0], hm_rs.at[0], tm=nxt)
    to_prev = rcopy(m_ref.at[0, pl.ds(0, PAD), lanes(c)], hm.at[1], hm_ss.at[1], hm_rs.at[1], tm=prv)
    to_next.start()
    to_prev.start()
    loads["k"].wait()
    kt = jnp.transpose(dot(normed, w_ref[1], 1, 0))
    for h in range(H):
        kh = kt[E * h : E * h + E]
        rad = jnp.sqrt(jnp.mean(kh * kh, axis=0, keepdims=True) + 1e-06)
        kh = kh / rad
        khat[h] = kh
        krad[h] = rad
        kvs[h, 0:E] = kh.astype(BF16)

    def send_all(lo, ss, rs):
        copies = []
        for o in (4, 3, 5, 2, 6, 1, 7):
            d = lax.rem(t + o, T)
            rows = pl.ds(lo, E)
            copies.append(
                rcopy(kvs.at[lax.rem(d, H), rows], kvr.at[t, rows], ss.at[o], rs.at[t], tm=d)
            )
            copies[-1].start()
        return copies

    kv_copies = send_all(0, k_ss, k_rs)
    loads["v"].wait()
    vt = jnp.transpose(dot(normed, w_ref[2], 1, 0))
    for h in range(H):
        kvs[h, E : 2 * E] = vt[E * h : E * h + E].astype(BF16)
    kv_copies += send_all(E, v_ss, v_rs)
    kvr[t] = kvs[p]

    loads["q"].wait()
    loads["sharp"].wait()
    qt = jnp.transpose(dot(normed, w_ref[0], 1, 0))
    for h in range(H):
        qh = qt[E * h : E * h + E]
        rad = jnp.sqrt(jnp.mean(qh * qh, axis=0, keepdims=True) + 1e-06)
        qh = qh / rad
        qhat[h] = qh
        qrad[h] = rad
        qs[h] = (qh * (sharp_ref[h] / math.sqrt(E))).astype(BF16)
    q_copies = []
    for o in range(1, H):
        d = lax.rem(p + o, H)
        q_copies.append(rcopy(qs.at[d], qr.at[p], q_ss.at[o], q_rs.at[o], tm=base + d))
        q_copies[-1].start()
    qr[p] = qs[p]

    loads["taps"].wait()
    to_next.wait_recv()
    to_prev.wait_recv()

    def fill(pad, halo, body):
        def one(i, carry):
            ln = pl.ds(pl.multiple_of(i * LANES, LANES), LANES)
            pad[i, 0:PAD, :] = jnp.where(t > 0, halo[0, :, ln].astype(F32), 0.0)
            pad[i, PAD + R : 2 * PAD + R, :] = jnp.where(t < T - 1, halo[1, :, ln].astype(F32), 0.0)
            body(i, ln)
            return carry

        lax.fori_loop(0, chunks, one, 0)

    def back(i, ln):
        mpad[i, PAD : PAD + R, :] = m_ref[0, :, lanes(c, i, LANES)].astype(F32)
        acc = mpad[i, PAD : PAD + R, :]
        for j in range(taps):
            s = PAD + reach - j
            acc = acc + taps_ref[j : j + 1, lanes(c, i, LANES)] * mpad[i, s : s + R, :]
        gres[c, :, ln] = acc.astype(BF16)

    fill(mpad, hm, back)
    gex = rcopy(gres.at[c], gres.at[c], ex_ss.at[0], ex_rs.at[0], mp=sib)
    gex.start()
    loads["fp"].wait()
    gex.wait_recv()
    gt = dot(fp_ref[:, 0:half], gres[0], 1, 1) + dot(fp_ref[:, half:D], gres[1], 1, 1)
    for h in range(H):
        gs[h] = gt[E * h : E * h + E].astype(BF16)
    g_copies = []
    for o in range(1, H):
        d = lax.rem(p + o, H)
        g_copies.append(rcopy(gs.at[d], gr.at[p], g_ss.at[o], g_rs.at[o], tm=base + d))
        g_copies[-1].start()
    gr[p] = gs[p]

    for cp in q_copies:
        cp.wait_recv()

    QT = jnp.concatenate([qr[i] for i in range(H)], axis=1)
    pairs = T // 2

    def pair(i, lo):
        return jnp.concatenate([kvr[2 * i, lo : lo + E], kvr[2 * i + 1, lo : lo + E]], axis=1)

    def arrived(i, lo, ss, rs):
        for e in range(2):
            src = 2 * i + e

            @pl.when(src != t)
            def _():
                rows = pl.ds(lo, E)
                rcopy(kvs.at[0, rows], kvr.at[src, rows], ss.at[0], rs.at[src], tm=nxt).wait_recv()

    def forward(n, state):
        total, att = state
        i = lax.rem(base // 2 + n, pairs)
        arrived(i, 0, k_ss, k_rs)
        w = jnp.exp(dot(pair(i, 0), QT, 0, 0))
        probs[i] = w
        arrived(i, E, v_ss, v_rs)
        return (
            total + jnp.sum(w, axis=0, keepdims=True),
            att + dot(pair(i, E), w.astype(BF16), 1, 0),
        )

    zero = jnp.zeros((1, H * R), F32)
    total, att = lax.fori_loop(0, pairs, forward, (zero, jnp.zeros((E, H * R), F32)))
    inv_total = 1.0 / total
    att = (att * inv_total).astype(BF16)
    for i in range(H):
        atts[i] = att[:, R * i : R * i + R]
    at_copies = []
    for o in range(1, H):
        d = lax.rem(p + o, H)
        at_copies.append(rcopy(atts.at[d], attr.at[p], at_ss.at[o], at_rs.at[o], tm=base + d))
        at_copies[-1].start()
    attr[p] = atts[p]

    for cp in g_copies:
        cp.wait_recv()
    GT = jnp.concatenate([gr[i] for i in range(H)], axis=1)

    def products(i, expect):
        prod = dot(pair(i, E), GT, 0, 0)
        prods[i] = prod
        return expect + jnp.sum(probs[i] * prod, axis=0, keepdims=True)

    expect = lax.fori_loop(0, pairs, products, zero)
    delta = expect * inv_total

    for cp in at_copies:
        cp.wait_recv()
    attended = attr[...].reshape(H * E, R)
    pos[...] = dot(attended, fp_ref[:, lanes(sib)], 0, 0).astype(BF16)
    pex = rcopy(pos, por, ex_ss.at[1], ex_rs.at[1], mp=sib)
    pex.start()

    def dk_copy(d):
        o = lax.rem(d + T - t, T)
        return rcopy(dkvs.at[d], dkvr.at[t], dk_ss.at[o], dk_rs.at[o], tm=d)

    def backward(n, dq):
        i = lax.rem(base // 2 + H // 2 + n, pairs)
        prob = probs[i] * inv_total
        slope = (prob * (prods[i] - delta)).astype(BF16)
        dk = dot(QT, slope, 1, 1).astype(BF16)
        dv = dot(GT, prob.astype(BF16), 1, 1).astype(BF16)
        for s in range(2):
            dkvs[2 * i + s, 0:E] = dk[:, R * s : R * s + R]
            dkvs[2 * i + s, E : 2 * E] = dv[:, R * s : R * s + R]
        return dq + dot(pair(i, 0), slope, 1, 0)

    far = pairs - H // 2
    dq = lax.fori_loop(0, far, backward, jnp.zeros((E, H * R), F32))
    own = x_ref[0, :, lanes(c)].astype(F32) + dot(attended, fp_ref[:, lanes(c)], 0, 0)
    pex.wait_recv()
    own = (own + por[...].astype(F32)).astype(BF16)
    resid[...] = own
    r_next = rcopy(resid.at[pl.ds(R - PAD, PAD)], hr.at[0], hr_ss.at[0], hr_rs.at[0], tm=nxt)
    r_prev = rcopy(resid.at[pl.ds(0, PAD)], hr.at[1], hr_ss.at[1], hr_rs.at[1], tm=prv)
    r_next.start()
    r_prev.start()


    def dk_send(n, carry):
        d = lax.rem(base + H + n, T)

        @pl.when(d != t)
        def _():
            dk_copy(d).start()

        return carry

    lax.fori_loop(0, T - H, dk_send, 0)
    dq = lax.fori_loop(far, pairs, backward, dq).astype(BF16)
    lax.fori_loop(T - H, T, dk_send, 0)
    for i in range(H):
        dqs[i] = dq[:, R * i : R * i + R]
    dk_copies = [dk_copy(lax.rem(t + o, T)) for o in range(1, T)]
    dkvr[t] = dkvs[t]
    dq_copies = []
    for o in range(1, H):
        d = lax.rem(p + o, H)
        dq_copies.append(rcopy(dqs.at[d], dqr.at[p], dq_ss.at[o], dq_rs.at[o], tm=base + d))
        dq_copies[-1].start()
    dqr[p] = dqs[p]

    r_next.wait_recv()
    r_prev.wait_recv()
    fl[taps:, :] = jnp.zeros((fl.shape[0] - taps, half), F32)

    def mix(i, ln):
        rpad[i, PAD : PAD + R, :] = resid[:, ln].astype(F32)
        grad = mpad[i, PAD : PAD + R, :]
        acc = rpad[i, PAD : PAD + R, :]
        for j in range(taps):
            s = PAD - reach + j
            win = rpad[i, s : s + R, :]
            acc = acc + taps_ref[j : j + 1, lanes(c, i, LANES)] * win
            fl[j : j + 1, ln] = jnp.sum(grad * win, axis=0, keepdims=True)
        sub_ref[0, :, lanes(c, i, LANES)] = acc.astype(BF16)

    fill(rpad, hr, mix)
    sex = rcopy(sub_ref.at[0, :, lanes(c)], sub_ref.at[0, :, lanes(c)], ex_ss.at[2], ex_rs.at[2], mp=sib)
    sex.start()

    width = filt_ref.shape[1]
    fs[...] = jnp.zeros(fs.shape, BF16)
    for k in range(T):
        fs[k, :, 0:width] = fl[:, width * k : width * k + width].astype(BF16)

    def filter_copy(k):
        return (
            jnp.logical_not((batch == c) & (t == k)),
            rcopy(fs.at[k], fr.at[flat], f_ss.at[k], f_rs.at[flat], batch=c, tm=k),
        )

    def filter_send(k, carry):
        away, cp = filter_copy(k)
        pl.when(away)(cp.start)
        return carry

    lax.fori_loop(0, T, filter_send, 0)

    @pl.when(batch == c)
    def _():
        fr[flat] = fs[t]

    for cp in dq_copies:
        cp.wait_recv()
    for cp in dk_copies:
        cp.wait_recv()
    parts = ([], [], [])
    for h in range(H):
        g = dqr[h].astype(F32) * (sharp_ref[h] / math.sqrt(E))
        hat = qhat[h]
        parts[0].append((g - hat * jnp.mean(g * hat, axis=0, keepdims=True)) / qrad[h])
        g = dkvr[h, 0:E].astype(F32)
        v = dkvr[h, E : 2 * E].astype(F32)
        for s in range(H, T, H):
            g = g + dkvr[s + h, 0:E].astype(F32)
            v = v + dkvr[s + h, E : 2 * E].astype(F32)
        hat = khat[h]
        parts[1].append((g - hat * jnp.mean(g * hat, axis=0, keepdims=True)) / krad[h])
        parts[2].append(v)
    rows = [jnp.transpose(jnp.concatenate(part, axis=0)).astype(BF16) for part in parts]
    n_copies = []
    for k in range(2):
        cols = slice(k * half, k * half + half)
        nps[k] = (
            dot(rows[0], w_ref[0, cols], 1, 1)
            + dot(rows[1], w_ref[1, cols], 1, 1)
            + dot(rows[2], w_ref[2, cols], 1, 1)
        ).astype(BF16)
        n_copies.append(rcopy(nps.at[k], npr.at[k], ex_ss.at[3 + k], ex_rs.at[3 + k], mp=sib))
        n_copies[-1].start()

    total_copy = rcopy(ft, ft, ex_ss.at[5], ex_rs.at[5], mp=sib)

    @pl.when(batch == c)
    def _():
        def filter_wait(i, carry):
            @pl.when(i != flat)
            def _():
                rcopy(fs.at[0], fr.at[i], f_ss.at[0], f_rs.at[i], tm=nxt).wait_recv()

            return carry

        lax.fori_loop(0, N, filter_wait, 0)
        acc = fr[0].astype(F32)
        for k in range(1, N):
            acc = acc + fr[k].astype(F32)
        ft[...] = acc
        total_copy.start()

    for cp in n_copies:
        cp.wait_recv()
    z = jnp.concatenate([nps[k].astype(F32) + npr[k].astype(F32) for k in range(2)], axis=1)
    u = unit[...]
    amp = jnp.sum(z * u, axis=0, keepdims=True)
    ams[...] = jnp.zeros(ams.shape, F32)
    for k in range(N):
        ams[k, 0:1, 0:width] = amp[:, width * k : width * k + width]

    def amp_copy(o):
        d = lax.rem(flat + o, N)
        return rcopy(ams.at[d], amr.at[flat], a_ss.at[o], a_rs.at[o], batch=d // T, tm=lax.rem(d, T))

    def amp_send(o, carry):
        amp_copy(o).start()
        return carry

    lax.fori_loop(1, N, amp_send, 0)
    amr[flat] = ams[flat]

    s = z * gain_ref[...].reshape(1, D)
    fb = (
        s - jnp.mean(s, axis=-1, keepdims=True) - u * jnp.mean(s * u, axis=-1, keepdims=True)
    ) * invstd[...]
    for k in range(2):
        cols = slice(k * half, k * half + half)
        sig_ref[0, :, cols] = (gres[k].astype(F32) + fb[:, cols]).astype(BF16)

    def amp_wait(o, carry):
        amp_copy(o).wait()
        return carry

    lax.fori_loop(1, N, amp_wait, 0)
    acc = amr[0]
    for k in range(1, N):
        acc = acc + amr[k]
    amp_ref[...] = acc[0:1, 0:width]

    @pl.when(batch == c)
    def _():
        total_copy.wait_send()

    @pl.when(batch != c)
    def _():
        total_copy.wait_recv()

    filt_ref[...] = ft[0:taps, 0:width]

    def filter_sent(k, carry):
        away, cp = filter_copy(k)
        pl.when(away)(cp.wait_send)
        return carry

    lax.fori_loop(0, T, filter_sent, 0)
    sex.wait_recv()
    for cp in (to_next, to_prev, r_next, r_prev, gex, pex, sex, *n_copies):
        cp.wait_send()
    for cp in kv_copies + q_copies + g_copies + at_copies + dq_copies + dk_copies:
        cp.wait_send()


def fused(x, gain, w, sharp, fp, taps, m):
    R, D = x.shape[1:]
    H = sharp.shape[0]
    E = w.shape[2] // H
    T = lax.axis_size("tm")
    N = T * lax.axis_size("batch")
    half = D // 2
    n_taps = taps.shape[0]
    width = D // N
    assert H * 2 == T and R == LANES
    v = pltpu.VMEM
    dma = pltpu.SemaphoreType.DMA
    vm = pl.BlockSpec(memory_space=pltpu.VMEM)
    hbm = pl.BlockSpec(memory_space=pltpu.HBM)
    sub, sig, filt, amp = pl.pallas_call(
        fused_kernel,
        out_shape=(
            jax.ShapeDtypeStruct((1, R, D), BF16),
            jax.ShapeDtypeStruct((1, R, D), BF16),
            jax.ShapeDtypeStruct((n_taps, width), F32),
            jax.ShapeDtypeStruct((1, width), F32),
        ),
        in_specs=[hbm] * 7,
        out_specs=(vm, vm, vm, vm),
        scratch_shapes=[
            v((R, D), F32), v((R, 1), F32), v((H, E, R), F32), v((H, E, R), F32),
            v((H, 1, R), F32), v((H, 1, R), F32),
            v((H, 2 * E, R), BF16), v((H, E, R), BF16), v((H, E, R), BF16),
            v((T, 2 * E, R), BF16), v((H, E, R), BF16), v((H, E, R), BF16),
            v((T // 2, 2 * R, H * R), F32), v((T // 2, 2 * R, H * R), F32),
            v((H, E, R), BF16), v((H, E, R), BF16), v((H, E, R), BF16), v((H, E, R), BF16),
            v((T, 2 * E, R), BF16), v((T, 2 * E, R), BF16),
            v((half // LANES, R + 2 * PAD, LANES), F32), v((half // LANES, R + 2 * PAD, LANES), F32),
            v((2, PAD, half), BF16), v((2, PAD, half), BF16),
            v((R, half), BF16), v((2, R, half), BF16),
            v((R, half), BF16), v((R, half), BF16), v((2, R, half), BF16), v((2, R, half), BF16),
            v((n_taps + 1, half), F32), v((T, n_taps + 1, LANES), BF16), v((N, n_taps + 1, LANES), BF16),
            v((n_taps + 1, LANES), F32), v((N, 1, LANES), F32), v((N, 1, LANES), F32),
            v((1, R, D), BF16), v((D,), F32), v(w.shape, BF16), pltpu.SMEM((H,), F32),
            v(fp.shape, BF16), v(taps.shape, F32), v((1, R, D), BF16), dma((9,)),
            dma((T,)), dma((T,)), dma((T,)), dma((T,)), dma((H,)), dma((H,)), dma((H,)), dma((H,)),
            dma((H,)), dma((H,)), dma((H,)), dma((H,)), dma((T,)), dma((T,)),
            dma((2,)), dma((2,)), dma((2,)), dma((2,)), dma((6,)), dma((6,)),
            dma((T,)), dma((N,)), dma((N,)), dma((N,)),
        ],
        compiler_params=pltpu.CompilerParams(
            collective_id=0, has_side_effects=True, vmem_limit_bytes=64 * 2**20 - 2**16
        ),
    )(x, gain, w, sharp, fp, taps, m)
    return sub, sig, filt, amp.reshape(width)


def solution(mesh):
    return jax.shard_map(
        fused if fits(mesh) else local,
        mesh=mesh,
        in_specs=(
            P("batch", "tm", None),
            P(),
            P(None, None, "mp"),
            P("mp"),
            P("mp", None),
            P(),
            P("batch", "tm", None),
        ),
        out_specs=(
            P("batch", "tm", None),
            P("batch", "tm", None),
            P(None, ("batch", "tm")),
            P(("batch", "tm")),
        ),
        check_vma=False,
    )
```
